512 devices in a mesh: train: 64 (over z_lo, y, x), feat: 8 (over z_hi, core).
Axes of the slice: x: 4, y: 8, z: 8 (z_hi: 4, z_lo: 2; z = z_hi * 2 + z_lo), core: 2. Of those that a mesh axis runs over, the one named last changes fastest.
Arguments:
- train_grads: bfloat16 [32768, 8192], P('train', 'feat'), may hold values from -0.0625 to 0.0625
- query_grads: bfloat16 [2048, 8192], P('train', 'feat'), may hold values from -6 to 6
- precond: bfloat16 [8192, 1024], P('feat'), may hold values from -0.5 to 4.5, as said below
Outputs:
- scores: float32 [32768, 2048], P('train', 'feat')
The draws below stay inside these ranges and needn't reach their ends.
Inputs may be any that keep to these rules, and one draw needn't show every extreme that they name: Each block of precond is symmetric.
All inputs are finite; a program needn't handle non-finite values.
Results may differ from the reference program's by a relative error of at most 0.0029.
Values may be sent and summed in bfloat16 or wider, within the bound.
A program may use at most 64 MiB of HBM per device.

```python
import jax
import jax.numpy as jnp
from jax import lax

K = 8192
BLK = 1024
ROWS = 32768
QUERIES = 2048


def draw_precond(key, part):
    key = jax.random.fold_in(key, 7)
    key_off = jax.random.fold_in(key, 1)
    key_diag = jax.random.fold_in(key, 2)
    blocks = K // BLK
    raw = jnp.clip(jax.random.normal(key_off, (blocks, BLK, BLK), jnp.float32), -4.0, 4.0)
    diag = jnp.exp(jax.random.uniform(key_diag, (blocks, BLK), jnp.float32, jnp.log(0.5), jnp.log(2.0)))
    off = (raw + jnp.swapaxes(raw, 1, 2)) * (0.35 / BLK ** 0.5)
    eye = jnp.eye(BLK, dtype=jnp.float32)
    full = off * (1.0 - eye) + diag[:, :, None] * eye
    return full.reshape(K, BLK).astype(jnp.bfloat16)


def levels(rng, dims, shards, least, largest):
    level = 1.0
    for position, blocks in shards:
        steps = jax.random.uniform(jax.random.fold_in(jax.random.fold_in(rng, 6), position), (blocks,), jnp.float32, least / len(shards), largest / len(shards))
        level = level * jnp.repeat(jnp.exp(steps), dims[position] // blocks).reshape((-1,) + (1,) * (len(dims) - 1 - position))
    return level


def normal_values(stream_key, extent, spread, reach, shards=(), kind=jnp.bfloat16):
    factor_of = levels(stream_key, extent, shards, -0.22, 0.18) if shards else 1.0
    array = jax.random.normal(stream_key, extent, jnp.float32) * spread * factor_of
    return jnp.minimum(jnp.maximum(array, -reach), reach).astype(kind)


def setup_inputs(seed: int = 0) -> dict:
    streams_of = jax.random.split(jax.random.key(seed), 4)
    return {
        "train_grads": normal_values(streams_of[0], (ROWS, K), K ** -0.5, 0.0625, ((0, 64), (1, 8))),
        "query_grads": normal_values(streams_of[1], (QUERIES, K), 1.0, 6.0, ((0, 64), (1, 8))),
        "precond": draw_precond(jax.random.fold_in(streams_of[3], 71), 0),
    }


def reference(train_grads, query_grads, precond):
    blocks = K // BLK
    queries = query_grads.astype(jnp.float32).reshape(QUERIES, blocks, BLK)
    inverse = precond.astype(jnp.float32).reshape(blocks, BLK, BLK)
    pre = jnp.einsum("qbi,bij->qbj", queries, inverse, precision=lax.Precision.HIGHEST)
    pre = pre.reshape(QUERIES, K).astype(jnp.bfloat16)
    return lax.dot_general(train_grads, pre, (((1,), (1,)), ((), ())), preferred_element_type=jnp.float32)
```

```python
import jax
import jax.numpy as jnp
from jax import lax
from jax.experimental import pallas as pl
from jax.experimental.pallas import tpu as pltpu
from jax.sharding import PartitionSpec as P

MESH = pl.DeviceIdType.MESH
XS, YS = 4, 8
ROWS, QROWS, W = 512, 32, 1024
CHUNK = XS * QROWS
KX = 768
XCOLS, YCOLS = pl.ds(0, KX), pl.ds(KX, 2 * W - KX)
NT = (((1,), (1,)), ((), ()))
X1, XY, YY, YX, Y2 = 0, 3, 35, 43, 59
N_TAGS = 75


def kernel(t_hbm, q_hbm, p_hbm, o_ref, prec, qry, pre, a, b, stage, lstage, local, parts,
           send, recv, load, init_s, init_r, a_s, a_r, rs_s, rs_r, l_s, l_r):
    t, f = lax.axis_index("train"), lax.axis_index("feat")
    x, y, zl = lax.rem(t, 4), lax.rem(t // 4, 8), t // 32
    zh, c = f // 2, lax.rem(f, 2)

    def dev(dx=0, dy=0, zlo=zl, zhi=zh, core=c):
        return (zlo * 32 + lax.rem(y + dy + 8, 8) * 4 + lax.rem(x + dx + 4, 4), zhi * 2 + core)

    def rows(dx=0, first=0, n=QROWS):
        return pl.ds(pl.multiple_of(lax.rem(x + dx + 4, 4) * QROWS + first, 16), n)

    def yi(dy):
        return lax.rem(y + dy + 8, 8)

    def panel(dy, dx, cols, first=0, n=QROWS):
        return b.at[yi(dy), rows(dx, first, n), cols]

    def copy(ref, tag, to):
        return pltpu.make_async_remote_copy(
            src_ref=ref, dst_ref=ref, send_sem=send.at[tag], recv_sem=recv.at[tag],
            device_id=to, device_id_type=MESH)

    started = []

    def go(ref, tag, to):
        cp = copy(ref, tag, to)
        cp.start()
        started.append(cp)

    def got(ref, tag):
        copy(ref, tag, dev()).wait_recv()

    half = pl.ds(pl.multiple_of(c * W, W), W)
    load_q = pltpu.make_async_copy(q_hbm, qry, load.at[0])
    load_p = pltpu.make_async_copy(p_hbm, prec, load.at[1])
    load_a = pltpu.make_async_copy(t_hbm, a.at[c], load.at[2])
    load_q.start()
    load_p.start()
    load_a.start()

    barrier = pltpu.get_barrier_semaphore()
    partners = [(t, lax.rem(f + i, 8)) for i in range(1, 8)]
    partners += [dev(dx=1), dev(dx=-1), dev(dx=2), dev(dy=1), dev(dy=-1)]
    partners += [dev(zlo=1 - zl, core=0), dev(zlo=1 - zl, core=1)]
    for partner in partners:
        pl.semaphore_signal(barrier, inc=1, device_id=partner, device_id_type=MESH)

    load_q.wait()
    load_p.wait()
    pre[...] = jnp.dot(qry[...], prec[...], preferred_element_type=jnp.float32).astype(jnp.bfloat16)
    pl.semaphore_wait(barrier, len(partners))

    mine = b.at[yi(0), rows(), half]

    def init(to, slot):
        return pltpu.make_async_remote_copy(
            src_ref=pre, dst_ref=mine, send_sem=init_s.at[slot], recv_sem=init_r.at[c],
            device_id=to, device_id_type=MESH)

    def init_got(h):
        dst = b.at[yi(0), rows(), pl.ds(pl.multiple_of(h * W, W), W)]
        pltpu.make_async_remote_copy(
            src_ref=pre, dst_ref=dst, send_sem=init_s.at[0], recv_sem=init_r.at[h],
            device_id=dev(), device_id_type=MESH).wait_recv()

    init_far = init(dev(zlo=1 - zl, core=zl), 0)
    init_near = init(dev(core=1 - c), 1)
    init_own = pltpu.make_async_copy(pre, mine, load.at[3])
    init_far.start()

    @pl.when(c == zl)
    def _():
        init_own.start()

    @pl.when(c != zl)
    def _():
        init_near.start()

    load_a.wait()
    a_copy = pltpu.make_async_remote_copy(
        src_ref=a.at[c], dst_ref=a.at[c], send_sem=a_s, recv_sem=a_r,
        device_id=dev(core=1 - c), device_id_type=MESH)
    a_copy.start()

    @pl.when(c == zl)
    def _():
        init_got(1 - c)
        init_own.wait()

    @pl.when(c != zl)
    def _():
        init_got(0)
        init_got(1)

    def chunk(i, dy):
        ys = yi(dy)
        acc = lax.dot_general(a[0], b[ys, :, pl.ds(0, W)], NT, preferred_element_type=jnp.float32)
        acc += lax.dot_general(a[1], b[ys, :, pl.ds(W, W)], NT, preferred_element_type=jnp.float32)
        owner, core, j = 2 * c + ys // 4, lax.rem(ys // 2, 2), lax.rem(ys, 2)

        @pl.when(owner != zh)
        def _():
            stage[i] = acc.astype(jnp.bfloat16)
            reduce_copy(i, dy).start()

        @pl.when(jnp.logical_and(owner == zh, core == c))
        def _():
            local[j] = acc

        @pl.when(jnp.logical_and(owner == zh, core != c))
        def _():
            lstage[j] = acc
            local_copy(j).start()

    def reduce_copy(i, dy):
        ys = yi(dy)
        owner, core, j = 2 * c + ys // 4, lax.rem(ys // 2, 2), lax.rem(ys, 2)
        slot = lax.rem(zh - owner + 3, 4)
        return pltpu.make_async_remote_copy(
            src_ref=stage.at[i], dst_ref=parts.at[slot, j], send_sem=rs_s.at[i], recv_sem=rs_r.at[slot, j],
            device_id=dev(zhi=owner, core=core), device_id_type=MESH)

    def local_copy(j):
        return pltpu.make_async_remote_copy(
            src_ref=lstage.at[j], dst_ref=local.at[j], send_sem=l_s.at[j], recv_sem=l_r.at[j],
            device_id=dev(core=1 - c), device_id_type=MESH)

    def chunks(k):
        def body(i, carry):
            chunk(2 * k - 1 + i, k * (1 - 2 * i))
            return carry
        lax.fori_loop(0, 2, body, 0)

    pieces = (0, 1, -1, 2)

    def xy_tag(d, k, p):
        return XY + (0 if d > 0 else 16) + k * 4 + p

    def xy_pieces(d, k):
        return range(4) if k < 3 else ((0, 3) if d > 0 else (1, 2))

    def xy_go(d, k, p):
        go(panel(-d * k, pieces[p], XCOLS), xy_tag(d, k, p), dev(dy=d))

    def xy_got(d, k, p):
        got(panel(-d * (k + 1), pieces[p], XCOLS), xy_tag(d, k, p))

    def yy_rows(d, k):
        return (0, QROWS) if k < 3 else ((0, 16) if d > 0 else (16, 16))

    def yy_go(d, k):
        go(panel(-d * k, 0, YCOLS, *yy_rows(d, k)), YY + (0 if d > 0 else 4) + k, dev(dy=d))

    def yy_got(d, k):
        got(panel(-d * (k + 1), 0, YCOLS, *yy_rows(d, k)), YY + (0 if d > 0 else 4) + k)

    def num(dy):
        return 0 if dy == 0 else 2 * abs(dy) - (1 if dy > 0 else 0)

    def yx_go(dy):
        for d in (1, -1):
            go(panel(dy, 0, YCOLS), YX + 2 * num(dy) + (0 if d > 0 else 1), dev(dx=d))

    def y2_forward(dy):
        for d in (1, -1):
            got(panel(dy, -d, YCOLS), YX + 2 * num(dy) + (0 if d > 0 else 1))
            first = 0 if d > 0 else 16
            go(panel(dy, -d, YCOLS, first, 16), Y2 + 2 * num(dy) + (0 if d > 0 else 1), dev(dx=d))

    def y2_got(dy):
        for d in (1, -1):
            first = 0 if d > 0 else 16
            got(panel(dy, 2, YCOLS, first, 16), Y2 + 2 * num(dy) + (0 if d > 0 else 1))

    def xy_stage(k):
        for d in (1, -1):
            for p in xy_pieces(d, k - 1):
                xy_got(d, k - 1, p)
                if k < 4 and p in xy_pieces(d, k):
                    xy_go(d, k, p)

    def yy_stage(k):
        for d in (1, -1):
            yy_got(d, k - 1)
            if k < 4:
                yy_go(d, k)
                yx_go(-d * k)
        if k == 4:
            yx_go(4)

    for d in (1, -1):
        yy_go(d, 0)
    for p in (1, 2, 3):
        go(panel(0, 0, XCOLS), X1 + p - 1, dev(dx=-pieces[p]))
    for d in (1, -1):
        xy_go(d, 0, 0)
    yx_go(0)
    yy_stage(1)
    for p in (1, 2, 3):
        got(panel(0, pieces[p], XCOLS), X1 + p - 1)
        for d in (1, -1):
            xy_go(d, 0, p)
    y2_forward(0)
    yy_stage(2)
    xy_stage(1)
    y2_got(0)
    a_copy.wait_recv()
    chunk(0, 0)
    for dy in (1, -1):
        y2_forward(dy)
    yy_stage(3)
    for dy in (1, -1):
        y2_got(dy)
    chunks(1)
    xy_stage(2)
    for dy in (2, -2):
        y2_forward(dy)
    yy_stage(4)
    for dy in (2, -2):
        y2_got(dy)
    chunks(2)
    xy_stage(3)
    for dy in (3, -3):
        y2_forward(dy)
    for dy in (3, -3):
        y2_got(dy)
    chunks(3)
    xy_stage(4)
    y2_forward(4)
    y2_got(4)
    chunk(7, 4)

    for cp in started:
        cp.wait_send()
    a_copy.wait_send()
    init_far.wait_send()

    @pl.when(c != zl)
    def _():
        init_near.wait_send()

    for i, dy in enumerate((0, 1, -1, 2, -2, 3, -3, 4)):
        @pl.when(2 * c + yi(dy) // 4 != zh)
        def _():
            reduce_copy(i, dy).wait_send()

    @pl.when(zh // 2 == c)
    def _():
        for j in range(2):
            local_copy(j).wait_send()

    @pl.when(zh // 2 != c)
    def _():
        for j in range(2):
            local_copy(j).wait_recv()

    for j in range(2):
        total = local[j]
        for slot in range(3):
            pltpu.make_async_remote_copy(
                src_ref=stage.at[0], dst_ref=parts.at[slot, j], send_sem=rs_s.at[0], recv_sem=rs_r.at[slot, j],
                device_id=dev(), device_id_type=MESH).wait_recv()
            total += parts[slot, j].astype(jnp.float32)
        o_ref[:, j * CHUNK:(j + 1) * CHUNK] = total


def body(train_grads, query_grads, precond):
    bf16, f32 = jnp.bfloat16, jnp.float32
    dma = pltpu.SemaphoreType.DMA
    return pl.pallas_call(
        kernel,
        out_shape=jax.ShapeDtypeStruct((ROWS, 2 * CHUNK), f32),
        in_specs=[pl.BlockSpec(memory_space=pl.ANY)] * 3,
        out_specs=pl.BlockSpec(memory_space=pltpu.VMEM),
        scratch_shapes=[
            pltpu.VMEM((W, W), bf16),
            pltpu.VMEM((QROWS, W), bf16),
            pltpu.VMEM((QROWS, W), bf16),
            pltpu.VMEM((2, ROWS, W), bf16),
            pltpu.VMEM((YS, CHUNK, 2 * W), bf16),
            pltpu.VMEM((YS, ROWS, CHUNK), bf16),
            pltpu.VMEM((2, ROWS, CHUNK), f32),
            pltpu.VMEM((2, ROWS, CHUNK), f32),
            pltpu.VMEM((3, 2, ROWS, CHUNK), bf16),
            dma((N_TAGS,)), dma((N_TAGS,)), dma((4,)), dma((2,)), dma((2,)), dma, dma,
            dma((YS,)), dma((3, 2)), dma((2,)), dma((2,)),
        ],
        compiler_params=pltpu.CompilerParams(
            collective_id=0, has_side_effects=True, vmem_limit_bytes=48 * 1024 * 1024),
        cost_estimate=pl.CostEstimate(flops=2 * 2 * W * W * ROWS, bytes_accessed=4 << 20, transcendentals=0),
    )(train_grads, query_grads, precond)


def solution(mesh):
    placed = (P("train", "feat"), P("train", "feat"), P("feat", None))
    return jax.shard_map(
        body, mesh=mesh, in_specs=placed, out_specs=P("train", "feat"), check_vma=False
    )
```

```python
import jax
import jax.numpy as jnp
from jax import lax
from jax.experimental import pallas as pl
from jax.experimental.pallas import tpu as pltpu
from jax.sharding import PartitionSpec as P

MESH = pl.DeviceIdType.MESH
XS, YS = 4, 8
ROWS, QROWS, W = 512, 32, 1024
CHUNK = XS * QROWS
KX = 896
XCOLS, YCOLS = pl.ds(0, KX), pl.ds(KX, 2 * W - KX)
NT = (((1,), (1,)), ((), ()))
HALF = ROWS // 2
DIRECT = (4,)
PIECES = (0, 1, -1, 2)
DISTANCES = (0, 1, -1, 2, -2, 3, -3, 4)
RATE, HOP, AHEAD, RELAY = 46500.0, 1.9, 2.0, 5.5


def pieces_of(d, k):
    return range(4) if k < 3 else ((0, 3) if d > 0 else (1, 2))


def messages():
    ky, out = 2 * W - KX, {}
    for d in (1, -1):
        xl, yl = ("x", d), ("y", d)
        for k in range(4):
            out["yy", d, k] = ([yl], QROWS if k < 3 else 16, ky, [("yy", d, k - 1)] if k else [], k)
            for p in pieces_of(d, k):
                needs = [("xy", d, k - 1, p)] if k else [("x1", p)] if p else []
                out["xy", d, k, p] = ([yl], QROWS, KX, needs, 2 + 2 * k + 0.1 * p)
        for dy in DISTANCES:
            needs = [] if dy == 0 else [("yy", 1, 3), ("yy", -1, 3)] if dy == 4 else [("yy", 1 if dy < 0 else -1, abs(dy) - 1)]
            late = 2 * abs(dy) + (0.5 if dy < 0 else 0)
            out["yx", dy, d] = ([xl], QROWS, ky, needs, 1 + late)
            out["y2", dy, d] = ([xl], 16, ky, [("yx", dy, d)], 2.2 + late)
    out["x1", 1] = ([("x", -1)], QROWS, KX, [], 0)
    out["x1", 2] = ([("x", 1)], QROWS, KX, [], 0)
    out["x1", 3] = ([("x", 1), ("x", -1)], QROWS, KX, [], 0)
    return out


def needs_of(dy):
    out = [(n, dy, d) for d in (1, -1) for n in ("yx", "y2")]
    if dy == 0:
        return out + [("x1", p) for p in (1, 2, 3)]
    if dy == 4:
        return out + [("xy", d, 3, p) for d in (1, -1) for p in pieces_of(d, 3)] + [("yy", 1, 3), ("yy", -1, 3)]
    d, k = 1 if dy < 0 else -1, abs(dy) - 1
    return out + [("xy", d, k, p) for p in range(4)] + [("yy", d, k)]


def plan():
    todo, here, free, steps = messages(), {}, {}, []
    while todo:
        best = None
        for name, (links, n, cols, needs, late) in todo.items():
            if all(q in here for q in needs):
                ready = max([here[q] for q in needs], default=0.0)
                start = max([ready] + [free.get(link, 0.0) for link in links])
                if best is None or (start, late) < best[:2]:
                    best = (start, late, name, ready)
        start, _, name, ready = best
        links, n, cols, needs, _ = todo.pop(name)
        end = start + n * cols * 2 / RATE
        free.update({link: end for link in links})
        here[name] = end + HOP + 0.5 * (len(links) - 1)
        steps.append((max(ready, start - AHEAD), len(steps), "go", name, needs))
    for dy in DISTANCES:
        at = max(here[q] for q in needs_of(dy))
        steps.append((at, len(steps), "chunk", dy, needs_of(dy)))
        if dy not in DIRECT:
            steps.append((at + RELAY, len(steps), "relay", dy, []))
    return [step[2:] for step in sorted(steps)]


def kernel(t_hbm, q_hbm, p_hbm, o_ref, prec, qry, pre, a, b, stage, hold, relay, lstage, local, parts,
           send, recv, load, init_s, init_r, a_s, a_r, rs_s, rs_r, mid_s, mid_r, l_s, l_r):
    t, f = lax.axis_index("train"), lax.axis_index("feat")
    x, y, zl = lax.rem(t, 4), lax.rem(t // 4, 8), t // 32
    zh, c = f // 2, lax.rem(f, 2)

    def dev(dx=0, dy=0, zlo=zl, zhi=zh, core=c):
        return (zlo * 32 + lax.rem(y + dy + 8, 8) * 4 + lax.rem(x + dx + 4, 4), zhi * 2 + core)

    def rows(dx=0, first=0, n=QROWS):
        return pl.ds(pl.multiple_of(lax.rem(x + dx + 4, 4) * QROWS + first, 16), n)

    def yi(dy):
        return lax.rem(y + dy + 8, 8)

    def panel(dy, dx, cols, first=0, n=QROWS):
        return b.at[yi(dy), rows(dx, first, n), cols]

    def copy(ref, tag, to):
        return pltpu.make_async_remote_copy(
            src_ref=ref, dst_ref=ref, send_sem=send.at[tag], recv_sem=recv.at[tag],
            device_id=to, device_id_type=MESH)

    started = []

    def go(ref, tag, to):
        cp = copy(ref, tag, to)
        cp.start()
        started.append(cp)

    def got(ref, tag):
        copy(ref, tag, dev()).wait_recv()

    half = pl.ds(pl.multiple_of(c * W, W), W)
    load_q = pltpu.make_async_copy(q_hbm, qry, load.at[0])
    load_p = pltpu.make_async_copy(p_hbm, prec, load.at[1])
    load_a = pltpu.make_async_copy(t_hbm, a.at[c], load.at[2])
    load_q.start()
    load_p.start()
    load_a.start()

    barrier = pltpu.get_barrier_semaphore()
    partners = [(t, lax.rem(f + i, 8)) for i in range(1, 8)]
    partners += [dev(dx=1), dev(dx=-1), dev(dx=2), dev(dy=1), dev(dy=-1)]
    partners += [dev(zlo=1 - zl, core=0), dev(zlo=1 - zl, core=1)]
    for partner in partners:
        pl.semaphore_signal(barrier, inc=1, device_id=partner, device_id_type=MESH)

    load_q.wait()
    load_p.wait()
    pre[...] = jnp.dot(qry[...], prec[...], preferred_element_type=jnp.float32).astype(jnp.bfloat16)
    pl.semaphore_wait(barrier, len(partners))

    mine = b.at[yi(0), rows(), half]

    def init(to, slot):
        return pltpu.make_async_remote_copy(
            src_ref=pre, dst_ref=mine, send_sem=init_s.at[slot], recv_sem=init_r.at[c],
            device_id=to, device_id_type=MESH)

    def init_got(h):
        dst = b.at[yi(0), rows(), pl.ds(pl.multiple_of(h * W, W), W)]
        pltpu.make_async_remote_copy(
            src_ref=pre, dst_ref=dst, send_sem=init_s.at[0], recv_sem=init_r.at[h],
            device_id=dev(), device_id_type=MESH).wait_recv()

    init_far = init(dev(zlo=1 - zl, core=zl), 0)
    init_near = init(dev(core=1 - c), 1)
    init_own = pltpu.make_async_copy(pre, mine, load.at[3])
    init_far.start()

    @pl.when(c == zl)
    def _():
        init_own.start()

    @pl.when(c != zl)
    def _():
        init_near.start()

    load_a.wait()
    a_copy = pltpu.make_async_remote_copy(
        src_ref=a.at[c], dst_ref=a.at[c], send_sem=a_s, recv_sem=a_r,
        device_id=dev(core=1 - c), device_id_type=MESH)
    a_copy.start()

    @pl.when(c == zl)
    def _():
        init_got(1 - c)
        init_own.wait()

    @pl.when(c != zl)
    def _():
        init_got(0)
        init_got(1)

    def place(dy):
        ys = yi(dy)
        owner = 2 * c + ys // 4
        return owner, lax.rem(ys // 2, 2), lax.rem(ys, 2), lax.rem(zh - owner + 4, 4)

    def owner_copy(i, dy, slot, h, kind):
        owner, core, j, _ = place(dy)
        part = pl.ds(0, ROWS) if h is None else pl.ds(pl.multiple_of(h * HALF, HALF), HALF)
        return pltpu.make_async_remote_copy(
            src_ref=stage.at[i, part], dst_ref=parts.at[slot, j, part], send_sem=rs_s.at[kind, i],
            recv_sem=rs_r.at[kind, slot, j], device_id=dev(zhi=owner, core=core), device_id_type=MESH)

    def relay_copy(i, h):
        return pltpu.make_async_remote_copy(
            src_ref=stage.at[i, pl.ds(h * HALF, HALF)], dst_ref=relay.at[i], send_sem=mid_s.at[h, i], recv_sem=mid_r.at[i],
            device_id=dev(zhi=lax.rem(zh + (3, 1)[h], 4)), device_id_type=MESH)

    def local_copy(j):
        return pltpu.make_async_remote_copy(
            src_ref=lstage.at[j], dst_ref=local.at[j], send_sem=l_s.at[j], recv_sem=l_r.at[j],
            device_id=dev(core=1 - c), device_id_type=MESH)

    def chunk(i, dy):
        ys = yi(dy)
        acc = lax.dot_general(a[0], b[ys, :, pl.ds(0, W)], NT, preferred_element_type=jnp.float32)
        acc += lax.dot_general(a[1], b[ys, :, pl.ds(W, W)], NT, preferred_element_type=jnp.float32)
        owner, core, j, away = place(dy)

        if dy in DIRECT:
            @pl.when(away != 0)
            def _():
                stage[i] = acc.astype(jnp.bfloat16)
                owner_copy(i, dy, away - 1, None, 2).start()
        else:
            @pl.when(away == 2)
            def _():
                stage[i] = acc.astype(jnp.bfloat16)
                relay_copy(i, 0).start()
                relay_copy(i, 1).start()

            for h, at in ((0, 1), (1, 3)):
                @pl.when(away == at)
                def _():
                    now = pl.ds((1 - h) * HALF, HALF)
                    stage[i, now] = acc[(1 - h) * HALF:(2 - h) * HALF].astype(jnp.bfloat16)
                    owner_copy(i, dy, h, 1 - h, 0).start()
                    hold[i] = acc[h * HALF:(h + 1) * HALF]

        @pl.when(jnp.logical_and(away == 0, core == c))
        def _():
            local[j] = acc

        @pl.when(jnp.logical_and(away == 0, core != c))
        def _():
            lstage[j] = acc
            local_copy(j).start()

    def relayed(i, dy):
        _, _, _, away = place(dy)

        @pl.when(lax.rem(away, 2) == 1)
        def _():
            h = away // 2
            relay_copy(i, 0).wait_recv()
            later = pl.ds(pl.multiple_of(h * HALF, HALF), HALF)
            stage[i, later] = (hold[i] + relay[i].astype(jnp.float32)).astype(jnp.bfloat16)
            owner_copy(i, dy, h, h, 1).start()

    tags = {name: n for n, name in enumerate(messages())}

    def message(name):
        kind = name[0]
        if kind == "x1":
            p = PIECES[name[1]]
            return (0, 0, XCOLS), (0, p, XCOLS), dev(dx=-p)
        if kind == "xy":
            _, d, k, p = name
            return (-d * k, PIECES[p], XCOLS), (-d * (k + 1), PIECES[p], XCOLS), dev(dy=d)
        if kind == "yy":
            _, d, k = name
            part = (0, QROWS) if k < 3 else (0, 16) if d > 0 else (16, 16)
            return (-d * k, 0, YCOLS, *part), (-d * (k + 1), 0, YCOLS, *part), dev(dy=d)
        _, dy, d = name
        part = (0, QROWS) if kind == "yx" else (0, 16) if d > 0 else (16, 16)
        hops = 0 if kind == "yx" else 1
        return (dy, -d * hops, YCOLS, *part), (dy, -d * (hops + 1), YCOLS, *part), dev(dx=d)

    seen = set()
    for kind, what, needs in plan():
        for name in needs:
            if name not in seen:
                seen.add(name)
                got(panel(*message(name)[1]), tags[name])
        if kind == "go":
            block, _, to = message(what)
            go(panel(*block), tags[what], to)
        elif kind == "chunk":
            if what == 0:
                a_copy.wait_recv()
            chunk(DISTANCES.index(what), what)
        else:
            relayed(DISTANCES.index(what), what)

    for cp in started:
        cp.wait_send()
    a_copy.wait_send()
    init_far.wait_send()

    @pl.when(c != zl)
    def _():
        init_near.wait_send()

    for i, dy in enumerate(DISTANCES):
        _, _, _, away = place(dy)
        if dy in DIRECT:
            @pl.when(away != 0)
            def _():
                owner_copy(i, dy, 0, None, 2).wait_send()
        else:
            @pl.when(away == 2)
            def _():
                relay_copy(i, 0).wait_send()
                relay_copy(i, 1).wait_send()

            @pl.when(lax.rem(away, 2) == 1)
            def _():
                owner_copy(i, dy, 0, 0, 0).wait_send()
                owner_copy(i, dy, 0, 0, 1).wait_send()

    @pl.when(zh // 2 == c)
    def _():
        for j in range(2):
            local_copy(j).wait_send()

    @pl.when(zh // 2 != c)
    def _():
        for j in range(2):
            local_copy(j).wait_recv()

    def part_got(slot, j, h, kind):
        part = pl.ds(0, ROWS) if h is None else pl.ds(h * HALF, HALF)
        pltpu.make_async_remote_copy(
            src_ref=stage.at[0, part], dst_ref=parts.at[slot, j, part], send_sem=rs_s.at[0, 0],
            recv_sem=rs_r.at[kind, slot, j], device_id=dev(), device_id_type=MESH).wait_recv()

    for j in range(2):
        away = lax.rem(4 * lax.rem(zh, 2) + 2 * c + j - y + 8, 8)
        straight = away == DIRECT[0] % 8
        for d in DIRECT[1:]:
            straight = jnp.logical_or(straight, away == d % 8)
        cols = slice(j * CHUNK, (j + 1) * CHUNK)

        @pl.when(straight)
        def _():
            for slot in range(3):
                part_got(slot, j, None, 2)
            o_ref[:, cols] = local[j] + sum(parts[slot, j].astype(jnp.float32) for slot in range(3))

        @pl.when(jnp.logical_not(straight))
        def _():
            for h in range(2):
                part_got(h, j, 1 - h, 0)
                part_got(h, j, h, 1)
            o_ref[:, cols] = local[j] + parts[0, j].astype(jnp.float32) + parts[1, j].astype(jnp.float32)


def body(train_grads, query_grads, precond):
    bf16, f32 = jnp.bfloat16, jnp.float32
    dma = pltpu.SemaphoreType.DMA
    n_tags = len(messages())
    return pl.pallas_call(
        kernel,
        out_shape=jax.ShapeDtypeStruct((ROWS, 2 * CHUNK), f32),
        in_specs=[pl.BlockSpec(memory_space=pltpu.HBM)] * 3,
        out_specs=pl.BlockSpec(memory_space=pltpu.VMEM),
        scratch_shapes=[
            pltpu.VMEM((W, W), bf16),
            pltpu.VMEM((QROWS, W), bf16),
            pltpu.VMEM((QROWS, W), bf16),
            pltpu.VMEM((2, ROWS, W), bf16),
            pltpu.VMEM((YS, CHUNK, 2 * W), bf16),
            pltpu.VMEM((YS, ROWS, CHUNK), bf16),
            pltpu.VMEM((YS, HALF, CHUNK), f32),
            pltpu.VMEM((YS, HALF, CHUNK), bf16),
            pltpu.VMEM((2, ROWS, CHUNK), f32),
            pltpu.VMEM((2, ROWS, CHUNK), f32),
            pltpu.VMEM((3, 2, ROWS, CHUNK), bf16),
            dma((n_tags,)), dma((n_tags,)), dma((4,)), dma((2,)), dma((2,)), dma, dma,
            dma((3, YS)), dma((3, 3, 2)), dma((2, YS)), dma((YS,)), dma((2,)), dma((2,)),
        ],
        compiler_params=pltpu.CompilerParams(
            collective_id=0, has_side_effects=True, vmem_limit_bytes=60 * 1024 * 1024),
        cost_estimate=pl.CostEstimate(flops=2 * 2 * W * W * ROWS, bytes_accessed=4 << 20, transcendentals=0),
    )(train_grads, query_grads, precond)


def solution(mesh):
    placed = (P("train", "feat"), P("train", "feat"), P("feat", None))
    return jax.shard_map(
        body, mesh=mesh, in_specs=placed, out_specs=P("train", "feat"), check_vma=False
    )
```

```python
import functools

import jax
import jax.numpy as jnp
from jax import lax
from jax.experimental import pallas as pl
from jax.experimental.pallas import tpu as pltpu
from jax.sharding import PartitionSpec as P

MESH = pl.DeviceIdType.MESH
XS, YS = 4, 8
ROWS, QROWS, W = 512, 32, 1024
CHUNK = XS * QROWS
KX = 896
XCOLS, YCOLS = pl.ds(0, KX), pl.ds(KX, 2 * W - KX)
NT = (((1,), (1,)), ((), ()))
HALF = ROWS // 2
DIRECT = ()
PIECES = (0, 1, -1, 2)
DISTANCES = (0, 1, -1, 2, -2, 3, -3, 4)
RATE, HOP, AHEAD, RELAY = 46500.0, 1.9, 2.0, 5.5


def pieces_of(k):
    return range(4) if k < 3 else range(2)


def messages():
    ky, out = 2 * W - KX, {}
    for d in (1, -1):
        xl, yl = ("x", d), ("y", d)
        for k in range(4):
            out["yy", d, k] = ([yl], QROWS if k < 3 else 16, ky, [("yy", d, k - 1)] if k else [], k)
            for p in pieces_of(k):
                needs = [("xy", d, 2, q) for q in range(4)] if k == 3 else [("xy", d, k - 1, p)] if k else [("x1", p)] if p else []
                out["xy", d, k, p] = ([yl], QROWS, KX, needs, 2 + 2 * k + 0.1 * p)
        for dy in DISTANCES:
            needs = [] if dy == 0 else [("yy", 1, 3), ("yy", -1, 3)] if dy == 4 else [("yy", 1 if dy < 0 else -1, abs(dy) - 1)]
            late = 2 * abs(dy) + (0.5 if dy < 0 else 0)
            out["yx", dy, d] = ([xl], QROWS, ky, needs, 1 + late)
            out["y2", dy, d] = ([xl], 16, ky, [("yx", dy, d)], 2.2 + late)
    out["x1", 1] = ([("x", -1)], QROWS, KX, [], 0)
    out["x1", 2] = ([("x", 1)], QROWS, KX, [], 0)
    out["x1", 3] = ([("x", 1), ("x", -1)], QROWS, KX, [], 0)
    return out


def needs_of(dy):
    out = [(n, dy, d) for d in (1, -1) for n in ("yx", "y2")]
    if dy == 0:
        return out + [("x1", p) for p in (1, 2, 3)]
    if dy == 4:
        return out + [("xy", d, 3, p) for d in (1, -1) for p in pieces_of(3)] + [("yy", 1, 3), ("yy", -1, 3)]
    d, k = 1 if dy < 0 else -1, abs(dy) - 1
    return out + [("xy", d, k, p) for p in range(4)] + [("yy", d, k)]


def plan():
    todo, here, free, steps = messages(), {}, {}, []
    while todo:
        best = None
        for name, (links, n, cols, needs, late) in todo.items():
            if all(q in here for q in needs):
                ready = max([here[q] for q in needs], default=0.0)
                start = max([ready] + [free.get(link, 0.0) for link in links])
                if best is None or (start, late) < best[:2]:
                    best = (start, late, name, ready)
        start, _, name, ready = best
        links, n, cols, needs, _ = todo.pop(name)
        end = start + n * cols * 2 / RATE
        free.update({link: end for link in links})
        here[name] = end + HOP + 0.5 * (len(links) - 1)
        steps.append((max(ready, start - AHEAD), len(steps), "go", name, needs))
    for dy in DISTANCES:
        at = max(here[q] for q in needs_of(dy))
        steps.append((at, len(steps), "chunk", dy, needs_of(dy)))
        if dy not in DIRECT:
            steps.append((at + RELAY, len(steps), "relay", dy, []))
    return [step[2:] for step in sorted(steps)]


def kernel(t_hbm, q_hbm, p_hbm, o_ref, prec, qry, pre, a, b, stage, hold, relay, lstage, local, parts,
           send, recv, load, init_s, init_r, a_s, a_r, rs_s, rs_r, mid_s, mid_r, l_s, l_r):
    t, f = lax.axis_index("train"), lax.axis_index("feat")
    x, y, zl = lax.rem(t, 4), lax.rem(t // 4, 8), t // 32
    zh, c = f // 2, lax.rem(f, 2)
    mirror = 2 * (lax.rem(y, 4) // 2) - 1

    def minus(d):
        return (1 - mirror * d) // 2

    def dev(dx=0, dy=0, zlo=zl, zhi=zh, core=c):
        return (zlo * 32 + lax.rem(y + dy + 8, 8) * 4 + lax.rem(x + dx + 4, 4), zhi * 2 + core)

    def rows(dx=0, first=0, n=QROWS):
        return pl.ds(pl.multiple_of(lax.rem(x + dx + 4, 4) * QROWS + first, 16), n)

    def yi(dy):
        return lax.rem(y + mirror * dy + 8, 8)

    def panel(dy, dx, cols, first=0, n=QROWS):
        return b.at[yi(dy), rows(dx, first, n), cols]

    def copy(ref, tag, to):
        return pltpu.make_async_remote_copy(
            src_ref=ref, dst_ref=ref, send_sem=send.at[tag], recv_sem=recv.at[tag],
            device_id=to, device_id_type=MESH)

    started = []

    def go(ref, tag, to):
        cp = copy(ref, tag, to)
        cp.start()
        started.append(cp)

    def got(ref, tag):
        copy(ref, tag, dev()).wait_recv()

    half = pl.ds(pl.multiple_of(c * W, W), W)
    load_q = pltpu.make_async_copy(q_hbm, qry, load.at[0])
    load_p = pltpu.make_async_copy(p_hbm, prec, load.at[1])
    load_a = pltpu.make_async_copy(t_hbm, a.at[c], load.at[2])
    load_q.start()
    load_p.start()
    load_a.start()

    barrier = pltpu.get_barrier_semaphore()
    partners = [(t, lax.rem(f + i, 8)) for i in range(1, 8)]
    partners += [dev(dx=1), dev(dx=-1), dev(dx=2), dev(dy=1), dev(dy=-1)]
    partners += [dev(zlo=1 - zl, core=0), dev(zlo=1 - zl, core=1)]
    for partner in partners:
        pl.semaphore_signal(barrier, inc=1, device_id=partner, device_id_type=MESH)

    load_q.wait()
    load_p.wait()
    pre[...] = jnp.dot(qry[...], prec[...], preferred_element_type=jnp.float32).astype(jnp.bfloat16)
    pl.semaphore_wait(barrier, len(partners))

    mine = b.at[yi(0), rows(), half]

    def init(to, slot):
        return pltpu.make_async_remote_copy(
            src_ref=pre, dst_ref=mine, send_sem=init_s.at[slot], recv_sem=init_r.at[c],
            device_id=to, device_id_type=MESH)

    def init_got(h):
        dst = b.at[yi(0), rows(), pl.ds(pl.multiple_of(h * W, W), W)]
        pltpu.make_async_remote_copy(
            src_ref=pre, dst_ref=dst, send_sem=init_s.at[0], recv_sem=init_r.at[h],
            device_id=dev(), device_id_type=MESH).wait_recv()

    init_far = init(dev(zlo=1 - zl, core=zl), 0)
    init_near = init(dev(core=1 - c), 1)
    init_own = pltpu.make_async_copy(pre, mine, load.at[3])
    init_far.start()

    @pl.when(c == zl)
    def _():
        init_own.start()

    @pl.when(c != zl)
    def _():
        init_near.start()

    load_a.wait()
    a_copy = pltpu.make_async_remote_copy(
        src_ref=a.at[c], dst_ref=a.at[c], send_sem=a_s, recv_sem=a_r,
        device_id=dev(core=1 - c), device_id_type=MESH)
    a_copy.start()

    @pl.when(c == zl)
    def _():
        init_got(1 - c)
        init_own.wait()

    @pl.when(c != zl)
    def _():
        init_got(0)
        init_got(1)

    def place(dy):
        ys = yi(dy)
        owner = 2 * c + ys // 4
        return owner, lax.rem(ys // 2, 2), lax.rem(ys, 2), lax.rem(zh - owner + 4, 4)

    def owner_copy(i, dy, slot, h, kind):
        owner, core, j, _ = place(dy)
        part = pl.ds(0, ROWS) if h is None else pl.ds(pl.multiple_of(h * HALF, HALF), HALF)
        return pltpu.make_async_remote_copy(
            src_ref=stage.at[i, part], dst_ref=parts.at[slot, j, part], send_sem=rs_s.at[kind, i],
            recv_sem=rs_r.at[kind, slot, j], device_id=dev(zhi=owner, core=core), device_id_type=MESH)

    def relay_copy(i, h):
        return pltpu.make_async_remote_copy(
            src_ref=stage.at[i, pl.ds(h * HALF, HALF)], dst_ref=relay.at[i], send_sem=mid_s.at[h, i], recv_sem=mid_r.at[i],
            device_id=dev(zhi=lax.rem(zh + (3, 1)[h], 4)), device_id_type=MESH)

    def local_copy(j):
        return pltpu.make_async_remote_copy(
            src_ref=lstage.at[j], dst_ref=local.at[j], send_sem=l_s.at[j], recv_sem=l_r.at[j],
            device_id=dev(core=1 - c), device_id_type=MESH)

    def chunk(i, dy):
        ys = yi(dy)
        acc = lax.dot_general(a[0], b[ys, :, pl.ds(0, W)], NT, preferred_element_type=jnp.float32)
        acc += lax.dot_general(a[1], b[ys, :, pl.ds(W, W)], NT, preferred_element_type=jnp.float32)
        owner, core, j, away = place(dy)

        if dy in DIRECT:
            @pl.when(away != 0)
            def _():
                stage[i] = acc.astype(jnp.bfloat16)
                owner_copy(i, dy, away - 1, None, 2).start()
        else:
            @pl.when(away == 2)
            def _():
                stage[i] = acc.astype(jnp.bfloat16)
                relay_copy(i, 0).start()
                relay_copy(i, 1).start()

            for h, at in ((0, 1), (1, 3)):
                @pl.when(away == at)
                def _():
                    now = pl.ds((1 - h) * HALF, HALF)
                    stage[i, now] = acc[(1 - h) * HALF:(2 - h) * HALF].astype(jnp.bfloat16)
                    owner_copy(i, dy, h, 1 - h, 0).start()
                    hold[i] = acc[h * HALF:(h + 1) * HALF]

        @pl.when(jnp.logical_and(away == 0, core == c))
        def _():
            local[j] = acc

        @pl.when(jnp.logical_and(away == 0, core != c))
        def _():
            lstage[j] = acc
            local_copy(j).start()

    def relayed(i, dy):
        _, _, _, away = place(dy)

        @pl.when(lax.rem(away, 2) == 1)
        def _():
            h = away // 2
            relay_copy(i, 0).wait_recv()
            later = pl.ds(pl.multiple_of(h * HALF, HALF), HALF)
            stage[i, later] = (hold[i] + relay[i].astype(jnp.float32)).astype(jnp.bfloat16)
            owner_copy(i, dy, h, h, 1).start()

    names = list(messages())
    per_way = [name for name in names if name[0] in ("yy", "xy") and name[1] > 0]
    rest = [name for name in names if name[0] not in ("yy", "xy")]

    def tag(name):
        if name[0] in ("yy", "xy"):
            return per_way.index((name[0], 1, *name[2:])) + len(per_way) * minus(name[1])
        return 2 * len(per_way) + rest.index(name)

    def message(name):
        kind = name[0]
        if kind == "x1":
            p = PIECES[name[1]]
            return (0, 0, XCOLS), (0, p, XCOLS), dev(dx=-p)
        if kind == "xy":
            _, d, k, p = name
            place_x = PIECES[p] if k < 3 else 2 * p + minus(d)
            return (-d * k, place_x, XCOLS), (-d * (k + 1), place_x, XCOLS), dev(dy=mirror * d)
        if kind == "yy":
            _, d, k = name
            part = (0, QROWS) if k < 3 else (16 * minus(d), 16)
            return (-d * k, 0, YCOLS, *part), (-d * (k + 1), 0, YCOLS, *part), dev(dy=mirror * d)
        _, dy, d = name
        part = (0, QROWS) if kind == "yx" else (0, 16) if d > 0 else (16, 16)
        hops = 0 if kind == "yx" else 1
        return (dy, -d * hops, YCOLS, *part), (dy, -d * (hops + 1), YCOLS, *part), dev(dx=d)

    seen = set()
    for kind, what, needs in plan():
        for name in needs:
            if name not in seen:
                seen.add(name)
                got(panel(*message(name)[1]), tag(name))
        if kind == "go":
            block, _, to = message(what)
            go(panel(*block), tag(what), to)
        elif kind == "chunk":
            if what == 0:
                a_copy.wait_recv()
            chunk(DISTANCES.index(what), what)
        else:
            relayed(DISTANCES.index(what), what)

    for cp in started:
        cp.wait_send()
    a_copy.wait_send()
    init_far.wait_send()

    @pl.when(c != zl)
    def _():
        init_near.wait_send()

    for i, dy in enumerate(DISTANCES):
        _, _, _, away = place(dy)
        if dy in DIRECT:
            @pl.when(away != 0)
            def _():
                owner_copy(i, dy, 0, None, 2).wait_send()
        else:
            @pl.when(away == 2)
            def _():
                relay_copy(i, 0).wait_send()
                relay_copy(i, 1).wait_send()

            @pl.when(lax.rem(away, 2) == 1)
            def _():
                owner_copy(i, dy, 0, 0, 0).wait_send()
                owner_copy(i, dy, 0, 0, 1).wait_send()

    @pl.when(zh // 2 == c)
    def _():
        for j in range(2):
            local_copy(j).wait_send()

    @pl.when(zh // 2 != c)
    def _():
        for j in range(2):
            local_copy(j).wait_recv()

    def part_got(slot, j, h, kind):
        part = pl.ds(0, ROWS) if h is None else pl.ds(h * HALF, HALF)
        pltpu.make_async_remote_copy(
            src_ref=stage.at[0, part], dst_ref=parts.at[slot, j, part], send_sem=rs_s.at[0, 0],
            recv_sem=rs_r.at[kind, slot, j], device_id=dev(), device_id_type=MESH).wait_recv()

    for j in range(2):
        dy = lax.rem(mirror * (4 * lax.rem(zh, 2) + 2 * c + j - y) + 16, 8)
        straight = functools.reduce(jnp.logical_or, [dy == d % 8 for d in DIRECT], dy < 0)
        cols = slice(j * CHUNK, (j + 1) * CHUNK)

        @pl.when(straight)
        def _():
            for slot in range(3):
                part_got(slot, j, None, 2)
            o_ref[:, cols] = local[j] + sum(parts[slot, j].astype(jnp.float32) for slot in range(3))

        @pl.when(jnp.logical_not(straight))
        def _():
            for h in range(2):
                part_got(h, j, 1 - h, 0)
                part_got(h, j, h, 1)
            o_ref[:, cols] = local[j] + parts[0, j].astype(jnp.float32) + parts[1, j].astype(jnp.float32)


def body(train_grads, query_grads, precond):
    bf16, f32 = jnp.bfloat16, jnp.float32
    dma = pltpu.SemaphoreType.DMA
    n_tags = len(messages())
    return pl.pallas_call(
        kernel,
        out_shape=pltpu.VMEM((ROWS, 2 * CHUNK), f32),
        in_specs=[pl.BlockSpec(memory_space=pltpu.HBM)] * 3,
        out_specs=pl.BlockSpec(memory_space=pltpu.VMEM),
        scratch_shapes=[
            pltpu.VMEM((W, W), bf16),
            pltpu.VMEM((QROWS, W), bf16),
            pltpu.VMEM((QROWS, W), bf16),
            pltpu.VMEM((2, ROWS, W), bf16),
            pltpu.VMEM((YS, CHUNK, 2 * W), bf16),
            pltpu.VMEM((YS, ROWS, CHUNK), bf16),
            pltpu.VMEM((YS, HALF, CHUNK), f32),
            pltpu.VMEM((YS, HALF, CHUNK), bf16),
            pltpu.VMEM((2, ROWS, CHUNK), f32),
            pltpu.VMEM((2, ROWS, CHUNK), f32),
            pltpu.VMEM((3, 2, ROWS, CHUNK), bf16),
            dma((n_tags,)), dma((n_tags,)), dma((4,)), dma((2,)), dma((2,)), dma, dma,
            dma((3, YS)), dma((3, 3, 2)), dma((2, YS)), dma((YS,)), dma((2,)), dma((2,)),
        ],
        compiler_params=pltpu.CompilerParams(
            collective_id=0, has_side_effects=True, vmem_limit_bytes=60 * 1024 * 1024),
        cost_estimate=pl.CostEstimate(flops=2 * 2 * W * W * ROWS, bytes_accessed=4 << 20, transcendentals=0),
    )(train_grads, query_grads, precond)


def solution(mesh):
    placed = (P("train", "feat"), P("train", "feat"), P("feat", None))
    return jax.shard_map(
        body, mesh=mesh, in_specs=placed, out_specs=P("train", "feat"), check_vma=False
    )
```

```python
import jax
import jax.numpy as jnp
from jax import lax
from jax.experimental import pallas as pl
from jax.experimental.pallas import tpu as pltpu
from jax.sharding import PartitionSpec as P

MESH = pl.DeviceIdType.MESH
XS, YS = 4, 8
ROWS, QROWS, W = 512, 32, 1024
CHUNK = XS * QROWS
KX = 896
XCOLS, YCOLS = pl.ds(0, KX), pl.ds(KX, 2 * W - KX)
NT = (((1,), (1,)), ((), ()))
PIECES = (0, 1, -1, 2)
DISTANCES = (0, 1, -1, 2, -2, 3, -3, 4)
UNITS = tuple((dy, None) for dy in DISTANCES[:-1]) + ((4, 0), (4, 1))
STRAIGHT = ()
RATE, HOP, AHEAD, RELAY = 46500.0, 1.9, 2.0, 6.2


def pieces_of(k):
    return range(4) if k < 3 else range(2)


def messages():
    ky, out = 2 * W - KX, {}
    for d in (1, -1):
        xl, yl = ("x", d), ("y", d)
        for k in range(4):
            out["yy", d, k] = ([yl], QROWS if k < 3 else 16, ky, [("yy", d, k - 1)] if k else [], k)
            for p in pieces_of(k):
                needs = [("xy", d, 2, q + p) for q in range(3)] if k == 3 else [("xy", d, k - 1, p)] if k else [("x1", p)] if p else []
                out["xy", d, k, p] = ([yl], QROWS, KX, needs, 2 + 2 * k + 0.1 * p)
        for dy in DISTANCES:
            needs = [] if dy == 0 else [("yy", 1, 3), ("yy", -1, 3)] if dy == 4 else [("yy", 1 if dy < 0 else -1, abs(dy) - 1)]
            late = 2 * abs(dy) + (0.5 if dy < 0 else 0)
            out["yx", dy, d] = ([xl], QROWS, ky, needs, 1 + late)
            out["y2", dy, d] = ([xl], 16, ky, [("yx", dy, d)], 2.2 + late)
    out["x1", 1] = ([("x", -1)], QROWS, KX, [], 0)
    out["x1", 2] = ([("x", 1)], QROWS, KX, [], 0)
    out["x1", 3] = ([("x", 1), ("x", -1)], QROWS, KX, [], 0)
    return out


def needs_of(dy, half=1):
    out = [("yx", dy, d) for d in (1, -1)] + [("y2", dy, d) for d in (1, -1) if half]
    if dy == 0:
        return out + [("x1", p) for p in (1, 2, 3)]
    if dy == 4:
        return out + [(n, d, 3, *q) for d in (1, -1) for n, q in [("yy", ())] + [("xy", (p,)) for p in range(half + 1)]]
    d, k = 1 if dy < 0 else -1, abs(dy) - 1
    return out + [("xy", d, k, p) for p in range(4)] + [("yy", d, k)]


def plan():
    todo, here, free, steps = messages(), {}, {}, []
    while todo:
        best = None
        for name, (links, n, cols, needs, late) in todo.items():
            if all(q in here for q in needs):
                ready = max([here[q] for q in needs], default=0.0)
                start = max([ready] + [free.get(link, 0.0) for link in links])
                if best is None or (start, late) < best[:2]:
                    best = (start, late, name, ready)
        start, _, name, ready = best
        links, n, cols, needs, _ = todo.pop(name)
        end = start + n * cols * 2 / RATE
        free.update({link: end for link in links})
        here[name] = end + HOP + 0.5 * (len(links) - 1)
        steps.append((max(ready, start - AHEAD), len(steps), "go", name, needs))
    for unit in UNITS:
        dy, half = unit
        needs = needs_of(dy) if half is None else needs_of(dy, half)
        at = max(here[q] for q in needs)
        steps.append((at, len(steps), "chunk", unit, needs))
        if unit not in STRAIGHT:
            steps.append((at + RELAY, len(steps), "relay", unit, []))
    steps.append((at, len(steps), "sent", None, []))
    return [step[2:] for step in sorted(steps)]


def kernel(t_hbm, q_hbm, p_hbm, o_ref, prec, qry, pre, a, b, stage, hold, relay, lstage, local, parts, lstage2, local2, parts2,
           send, recv, load, init_s, init_r, a_s, a_r, rs_s, rs_r, rs2_r, mid_s, mid_r, l_s, l_r):
    t, f = lax.axis_index("train"), lax.axis_index("feat")
    x, y, zl = lax.rem(t, 4), lax.rem(t // 4, 8), t // 32
    zh, c = f // 2, lax.rem(f, 2)
    serves = lax.rem(c + zl, 2)
    mirror = 2 * (lax.rem(y, 4) // 2) - 1

    def minus(d):
        return (1 - mirror * d) // 2

    def dev(dx=0, dy=0, zlo=zl, zhi=zh, core=c):
        return (zlo * 32 + lax.rem(y + dy + 8, 8) * 4 + lax.rem(x + dx + 4, 4), zhi * 2 + core)

    def rows(dx=0, first=0, n=QROWS):
        return pl.ds(pl.multiple_of(lax.rem(x + dx + 4, 4) * QROWS + first, 16), n)

    def yi(dy):
        return lax.rem(y + mirror * dy + 8, 8)

    def panel(dy, dx, cols, first=0, n=QROWS):
        return b.at[yi(dy), rows(dx, first, n), cols]

    def copy(ref, tag, to):
        return pltpu.make_async_remote_copy(
            src_ref=ref, dst_ref=ref, send_sem=send.at[tag], recv_sem=recv.at[tag],
            device_id=to, device_id_type=MESH)

    started = []

    def go(ref, tag, to):
        cp = copy(ref, tag, to)
        cp.start()
        started.append(cp)

    def got(ref, tag):
        copy(ref, tag, dev()).wait_recv()

    half = pl.ds(pl.multiple_of(c * W, W), W)
    load_q = pltpu.make_async_copy(q_hbm, qry, load.at[0])
    load_p = pltpu.make_async_copy(p_hbm, prec, load.at[1])
    load_a = pltpu.make_async_copy(t_hbm, a.at[c], load.at[2])
    load_q.start()
    load_p.start()
    load_a.start()

    barrier = pltpu.get_barrier_semaphore()
    partners = [dev(zhi=lax.rem(zh + i, 4), core=k) for i in (1, 3) for k in range(2)] + [dev(core=1 - c)]
    partners += [dev(dx=1), dev(dx=-1), dev(dx=2), dev(dy=1), dev(dy=-1)]
    partners += [dev(zlo=1 - zl, core=0), dev(zlo=1 - zl, core=1)]
    for partner in partners:
        pl.semaphore_signal(barrier, inc=1, device_id=partner, device_id_type=MESH)

    load_q.wait()
    load_p.wait()
    pre[...] = jnp.dot(qry[...], prec[...], preferred_element_type=jnp.float32).astype(jnp.bfloat16)
    pl.semaphore_wait(barrier, len(partners))

    mine = b.at[yi(0), rows(), half]

    def init(to, slot):
        return pltpu.make_async_remote_copy(
            src_ref=pre, dst_ref=mine, send_sem=init_s.at[slot], recv_sem=init_r.at[c],
            device_id=to, device_id_type=MESH)

    def init_got(h):
        dst = b.at[yi(0), rows(), pl.ds(pl.multiple_of(h * W, W), W)]
        pltpu.make_async_remote_copy(
            src_ref=pre, dst_ref=dst, send_sem=init_s.at[0], recv_sem=init_r.at[h],
            device_id=dev(), device_id_type=MESH).wait_recv()

    init_far = init(dev(zlo=1 - zl, core=1), 0)
    init_near = init(dev(core=1 - c), 1)
    init_own = pltpu.make_async_copy(pre, mine, load.at[3])
    init_far.start()

    @pl.when(c == 0)
    def _():
        init_own.start()

    @pl.when(c != 0)
    def _():
        init_near.start()

    load_a.wait()
    a_copy = pltpu.make_async_remote_copy(
        src_ref=a.at[c], dst_ref=a.at[c], send_sem=a_s, recv_sem=a_r,
        device_id=dev(core=1 - c), device_id_type=MESH)
    a_copy.start()

    @pl.when(c == 0)
    def _():
        init_got(1)
        init_own.wait()

    @pl.when(c != 0)
    def _():
        init_got(0)
        init_got(1)

    def place(dy):
        ys = yi(dy)
        owner = 2 * serves + ys // 4
        return owner, lax.rem(ys // 2, 2), lax.rem(ys, 2), lax.rem(zh - owner + 4, 4)

    def height(unit):
        return ROWS if unit[1] is None else ROWS // 2

    def landing(unit, slot, j, part, kind):
        if unit[1] is None:
            return parts.at[slot, j, part], rs_r.at[kind, slot, j]
        return parts2.at[slot, unit[1], part], rs2_r.at[kind, slot, unit[1]]

    def part_of(unit, h):
        n = height(unit)
        return pl.ds(0, n) if h is None else pl.ds(pl.multiple_of(h * (n // 2), n // 2), n // 2)

    def owner_copy(unit, slot, h, kind):
        owner, core, j, _ = place(unit[0])
        i, part = UNITS.index(unit), part_of(unit, h)
        dst, sem = landing(unit, slot, j, part, kind)
        return pltpu.make_async_remote_copy(
            src_ref=stage.at[i, part], dst_ref=dst, send_sem=rs_s.at[kind, i], recv_sem=sem,
            device_id=dev(zhi=owner, core=core), device_id_type=MESH)

    def relay_copy(unit, h):
        i = UNITS.index(unit)
        return pltpu.make_async_remote_copy(
            src_ref=stage.at[i, part_of(unit, h)], dst_ref=relay.at[i, pl.ds(0, height(unit) // 2)],
            send_sem=mid_s.at[h, i], recv_sem=mid_r.at[i],
            device_id=dev(zhi=lax.rem(zh + (3, 1)[h], 4)), device_id_type=MESH)

    def local_copy(half, j):
        src, dst, k = (lstage.at[j], local.at[j], j) if half is None else (lstage2.at[half], local2.at[half], 2 + half)
        return pltpu.make_async_remote_copy(
            src_ref=src, dst_ref=dst, send_sem=l_s.at[k], recv_sem=l_r.at[k],
            device_id=dev(core=1 - c), device_id_type=MESH)

    def pair(half):
        low = x // 2 if half == 0 else 1 - x // 2
        return pl.ds(pl.multiple_of(low * CHUNK // 2, CHUNK // 2), CHUNK // 2)

    def chunk(unit):
        dy, half = unit
        i, n, ys = UNITS.index(unit), height(unit), yi(dy)
        these = slice(None) if half is None else pair(half)
        acc = lax.dot_general(a[0], b[ys, these, pl.ds(0, W)], NT, preferred_element_type=jnp.float32)
        acc += lax.dot_general(a[1], b[ys, these, pl.ds(W, W)], NT, preferred_element_type=jnp.float32)
        if half is not None:
            acc = jnp.concatenate([acc[:n], acc[n:]], axis=1)
        owner, core, j, away = place(dy)

        if unit in STRAIGHT:
            @pl.when(away != 0)
            def _():
                stage[i, :n] = acc.astype(jnp.bfloat16)
                owner_copy(unit, away - 1, None, 2).start()
        else:
            @pl.when(away == 2)
            def _():
                stage[i, :n] = acc.astype(jnp.bfloat16)
                relay_copy(unit, 0).start()
                relay_copy(unit, 1).start()

            for h, at in ((0, 1), (1, 3)):
                @pl.when(away == at)
                def _():
                    stage[i, part_of(unit, 1 - h)] = acc[(1 - h) * (n // 2):(2 - h) * (n // 2)].astype(jnp.bfloat16)
                    owner_copy(unit, 2 * h, 1 - h, 0).start()
                    hold[i, :n // 2] = acc[h * (n // 2):(h + 1) * (n // 2)]

        @pl.when(jnp.logical_and(away == 0, core == c))
        def _():
            if half is None:
                local[j] = acc
            else:
                local2[half] = acc

        @pl.when(jnp.logical_and(away == 0, core != c))
        def _():
            if half is None:
                lstage[j] = acc
            else:
                lstage2[half] = acc
            local_copy(half, j).start()

    def relayed(unit):
        i, n = UNITS.index(unit), height(unit)
        _, _, _, away = place(unit[0])

        @pl.when(lax.rem(away, 2) == 1)
        def _():
            h = away // 2
            relay_copy(unit, 0).wait_recv()
            stage[i, part_of(unit, h)] = (hold[i, :n // 2] + relay[i, :n // 2].astype(jnp.float32)).astype(jnp.bfloat16)
            owner_copy(unit, 2 * h, h, 1).start()

    names = list(messages())
    per_way = [name for name in names if name[0] in ("yy", "xy") and name[1] > 0]
    rest = [name for name in names if name[0] not in ("yy", "xy")]

    def tag(name):
        if name[0] in ("yy", "xy"):
            return per_way.index((name[0], 1, *name[2:])) + len(per_way) * minus(name[1])
        return 2 * len(per_way) + rest.index(name)

    def message(name):
        kind = name[0]
        if kind == "x1":
            p = PIECES[name[1]]
            return (0, 0, XCOLS), (0, p, XCOLS), dev(dx=-p)
        if kind == "xy":
            _, d, k, p = name
            place_x = PIECES[p] if k < 3 else (1 - minus(d)) * 2 * p + minus(d) * (1 - 2 * p) * (1 - 2 * lax.rem(x, 2))
            return (-d * k, place_x, XCOLS), (-d * (k + 1), place_x, XCOLS), dev(dy=mirror * d)
        if kind == "yy":
            _, d, k = name
            part = (0, QROWS) if k < 3 else (16 * minus(d), 16)
            return (-d * k, 0, YCOLS, *part), (-d * (k + 1), 0, YCOLS, *part), dev(dy=mirror * d)
        _, dy, d = name
        part = (0, QROWS) if kind == "yx" else (0, 16) if d > 0 else (16, 16)
        hops = 0 if kind == "yx" else 1
        return (dy, -d * hops, YCOLS, *part), (dy, -d * (hops + 1), YCOLS, *part), dev(dx=d)

    def sent():
        for cp in started:
            cp.wait_send()
        a_copy.wait_send()
        init_far.wait_send()

        @pl.when(c != 0)
        def _():
            init_near.wait_send()

    seen = set()
    for kind, what, needs in plan():
        for name in needs:
            if name not in seen:
                seen.add(name)
                got(panel(*message(name)[1]), tag(name))
        if kind == "go":
            block, _, to = message(what)
            go(panel(*block), tag(what), to)
        elif kind == "chunk":
            if what == UNITS[0]:
                a_copy.wait_recv()
            chunk(what)
        elif kind == "relay":
            relayed(what)
        else:
            sent()

    for unit in UNITS:
        _, _, j, away = place(unit[0])
        if unit in STRAIGHT:
            @pl.when(away != 0)
            def _():
                owner_copy(unit, 0, None, 2).wait_send()
        else:
            @pl.when(away == 2)
            def _():
                relay_copy(unit, 0).wait_send()
                relay_copy(unit, 1).wait_send()

            @pl.when(lax.rem(away, 2) == 1)
            def _():
                owner_copy(unit, 0, 0, 0).wait_send()
                owner_copy(unit, 0, 0, 1).wait_send()

        _, core, j, _ = place(unit[0])

        @pl.when(jnp.logical_and(away == 0, core != c))
        def _():
            local_copy(unit[1], j).wait_send()

    def part_got(unit, slot, j, h, kind):
        part = part_of(unit, h)
        dst, sem = landing(unit, slot, j, part, kind)
        pltpu.make_async_remote_copy(
            src_ref=stage.at[0, part], dst_ref=dst, send_sem=rs_s.at[0, 0], recv_sem=sem,
            device_id=dev(), device_id_type=MESH).wait_recv()

    def collect(unit, j):
        @pl.when(zh // 2 != serves)
        def _():
            local_copy(unit[1], j).wait_recv()

        if unit in STRAIGHT:
            for slot in range(3):
                part_got(unit, slot, j, None, 2)
        else:
            for h in range(2):
                part_got(unit, 2 * h, j, 1 - h, 0)
                part_got(unit, 2 * h, j, h, 1)
        own, come = (local[j], parts.at[:, j]) if unit[1] is None else (local2[unit[1]], parts2.at[:, unit[1]])
        return own + sum(come[slot].astype(jnp.float32) for slot in ((0, 1, 2) if unit in STRAIGHT else (0, 2)))

    for j in range(2):
        far = lax.rem(4 * lax.rem(zh, 2) + 2 * c + j - y + 8, 8) == 4
        cols = slice(j * CHUNK, (j + 1) * CHUNK)

        @pl.when(jnp.logical_not(far))
        def _():
            o_ref[:, cols] = collect(UNITS[0], j)

        @pl.when(far)
        def _():
            mine, other = collect((4, 0), j), collect((4, 1), j)
            first = x // 2 == 0
            left, right = jnp.where(first, mine, other), jnp.where(first, other, mine)
            half = CHUNK // 2
            o_ref[:ROWS // 2, cols] = jnp.concatenate([left[:, :half], right[:, :half]], axis=1)
            o_ref[ROWS // 2:, cols] = jnp.concatenate([left[:, half:], right[:, half:]], axis=1)


def body(train_grads, query_grads, precond):
    bf16, f32 = jnp.bfloat16, jnp.float32
    dma = pltpu.SemaphoreType.DMA
    n_tags = len(messages())
    return pl.pallas_call(
        kernel,
        out_shape=pltpu.VMEM((ROWS, 2 * CHUNK), f32),
        in_specs=[pl.BlockSpec(memory_space=pltpu.HBM)] * 3,
        out_specs=pl.BlockSpec(memory_space=pltpu.VMEM),
        scratch_shapes=[
            pltpu.VMEM((W, W), bf16),
            pltpu.VMEM((QROWS, W), bf16),
            pltpu.VMEM((QROWS, W), bf16),
            pltpu.VMEM((2, ROWS, W), bf16),
            pltpu.VMEM((YS, CHUNK, 2 * W), bf16),
            pltpu.VMEM((len(UNITS), ROWS, CHUNK), bf16),
            pltpu.VMEM((len(UNITS), ROWS // 2, CHUNK), f32),
            pltpu.VMEM((len(UNITS), ROWS // 2, CHUNK), bf16),
            pltpu.VMEM((2, ROWS, CHUNK), f32),
            pltpu.VMEM((2, ROWS, CHUNK), f32),
            pltpu.VMEM((3, 2, ROWS, CHUNK), bf16),
            pltpu.VMEM((2, ROWS // 2, CHUNK), f32),
            pltpu.VMEM((2, ROWS // 2, CHUNK), f32),
            pltpu.VMEM((3, 2, ROWS // 2, CHUNK), bf16),
            dma((n_tags,)), dma((n_tags,)), dma((4,)), dma((2,)), dma((2,)), dma, dma,
            dma((3, len(UNITS))), dma((2, 3, 2)), dma((3, 3, 2)), dma((2, len(UNITS))), dma((len(UNITS),)), dma((4,)), dma((4,)),
        ],
        compiler_params=pltpu.CompilerParams(
            collective_id=0, has_side_effects=True, vmem_limit_bytes=60 * 1024 * 1024),
        cost_estimate=pl.CostEstimate(flops=2 * 2 * W * W * ROWS, bytes_accessed=4 << 20, transcendentals=0),
    )(train_grads, query_grads, precond)


def solution(mesh):
    placed = (P("train", "feat"), P("train", "feat"), P("feat", None))
    return jax.shard_map(
        body, mesh=mesh, in_specs=placed, out_specs=P("train", "feat"), check_vma=False
    )
```

```python
import jax
import jax.numpy as jnp
from jax import lax
from jax.experimental import pallas as pl
from jax.experimental.pallas import tpu as pltpu
from jax.sharding import PartitionSpec as P

MESH = pl.DeviceIdType.MESH
XS, YS = 4, 8
ROWS, QROWS, W = 512, 32, 1024
CHUNK = XS * QROWS
KX = 896
XCOLS, YCOLS = pl.ds(0, KX), pl.ds(KX, 2 * W - KX)
NT = (((1,), (1,)), ((), ()))
PIECES = (0, 1, -1, 2)
DISTANCES = (0, 1, -1, 2, -2, 3, -3, 4)
UNITS = tuple((dy, None) for dy in DISTANCES[:-1]) + ((4, 0), (4, 1))
STRAIGHT = ()
RATE, HOP, AHEAD, RELAY = 46500.0, 1.9, 2.0, 6.2


def pieces_of(k):
    return range(4) if k < 3 else range(2)


def messages():
    ky, out = 2 * W - KX, {}
    for d in (1, -1):
        xl, yl = ("x", d), ("y", d)
        for k in range(4):
            out["yy", d, k] = ([yl], QROWS if k < 3 else 16, ky, [("yy", d, k - 1)] if k else [], k)
            for p in pieces_of(k):
                needs = [("xy", d, 2, q + p) for q in range(3)] if k == 3 else [("xy", d, k - 1, p)] if k else [("x1", p)] if p else []
                out["xy", d, k, p] = ([yl], QROWS, KX, needs, 2 + 2 * k + 0.1 * p)
        for dy in DISTANCES:
            needs = [] if dy == 0 else [("yy", 1, 3), ("yy", -1, 3)] if dy == 4 else [("yy", 1 if dy < 0 else -1, abs(dy) - 1)]
            late = 2 * abs(dy) + (0.5 if dy < 0 else 0)
            out["yx", dy, d] = ([xl], QROWS, ky, needs, 1 + late)
            out["y2", dy, d] = ([xl], 16, ky, [("yx", dy, d)], 2.2 + late)
    out["x1", 1] = ([("x", -1)], QROWS, KX, [], 0)
    out["x1", 2] = ([("x", 1)], QROWS, KX, [], 0)
    out["x1", 3] = ([("x", 1), ("x", -1)], QROWS, KX, [], 0)
    return out


def needs_of(dy, half=1):
    out = [("yx", dy, d) for d in (1, -1)] + [("y2", dy, d) for d in (1, -1) if half]
    if dy == 0:
        return out + [("x1", p) for p in (1, 2, 3)]
    if dy == 4:
        return out + [(n, d, 3, *q) for d in (1, -1) for n, q in [("yy", ())] + [("xy", (p,)) for p in range(half + 1)]]
    d, k = 1 if dy < 0 else -1, abs(dy) - 1
    return out + [("xy", d, k, p) for p in range(4)] + [("yy", d, k)]


def plan():
    todo, here, free, steps = messages(), {}, {}, []
    while todo:
        best = None
        for name, (links, n, cols, needs, late) in todo.items():
            if all(q in here for q in needs):
                ready = max([here[q] for q in needs], default=0.0)
                start = max([ready] + [free.get(link, 0.0) for link in links])
                if best is None or (start, late) < best[:2]:
                    best = (start, late, name, ready)
        start, _, name, ready = best
        links, n, cols, needs, _ = todo.pop(name)
        end = start + n * cols * 2 / RATE
        free.update({link: end for link in links})
        here[name] = end + HOP + 0.5 * (len(links) - 1)
        steps.append((max(ready, start - AHEAD), len(steps), "go", name, needs))
    for unit in UNITS:
        dy, half = unit
        needs = needs_of(dy) if half is None else needs_of(dy, half)
        at = max(here[q] for q in needs)
        steps.append((at, len(steps), "chunk", unit, needs))
        if unit not in STRAIGHT:
            steps.append((at + (RELAY if abs(dy) < 3 else 4.0), len(steps), "relay", unit, []))
    steps.append((at, len(steps), "sent", None, []))
    return [step[2:] for step in sorted(steps)]


def kernel(t_hbm, q_hbm, p_hbm, o_ref, prec, qry, pre, a, b, stage, hold, relay, lstage, local, parts, lstage2, local2, parts2,
           send, recv, load, init_s, init_r, a_s, a_r, rs_s, rs_r, rs2_r, mid_s, mid_r, l_s, l_r):
    t, f = lax.axis_index("train"), lax.axis_index("feat")
    x, y, zl = lax.rem(t, 4), lax.rem(t // 4, 8), t // 32
    zh, c = f // 2, lax.rem(f, 2)
    serves = lax.rem(c + zl, 2)
    mirror = 2 * (lax.rem(y, 4) // 2) - 1

    def minus(d):
        return (1 - mirror * d) // 2

    def dev(dx=0, dy=0, zlo=zl, zhi=zh, core=c):
        return (zlo * 32 + lax.rem(y + dy + 8, 8) * 4 + lax.rem(x + dx + 4, 4), zhi * 2 + core)

    def rows(dx=0, first=0, n=QROWS):
        return pl.ds(pl.multiple_of(lax.rem(x + dx + 4, 4) * QROWS + first, 16), n)

    def yi(dy):
        return lax.rem(y + mirror * dy + 8, 8)

    def panel(dy, dx, cols, first=0, n=QROWS):
        return b.at[yi(dy), rows(dx, first, n), cols]

    def copy(ref, tag, to):
        return pltpu.make_async_remote_copy(
            src_ref=ref, dst_ref=ref, send_sem=send.at[tag], recv_sem=recv.at[tag],
            device_id=to, device_id_type=MESH)

    started = []

    def go(ref, tag, to):
        cp = copy(ref, tag, to)
        cp.start()
        started.append(cp)

    def got(ref, tag):
        copy(ref, tag, dev()).wait_recv()

    half = pl.ds(pl.multiple_of(c * W, W), W)
    load_q = pltpu.make_async_copy(q_hbm, qry, load.at[0])
    load_p = pltpu.make_async_copy(p_hbm, prec, load.at[1])
    load_a = pltpu.make_async_copy(t_hbm, a.at[c], load.at[2])
    load_q.start()
    load_p.start()
    load_a.start()

    barrier = pltpu.get_barrier_semaphore()
    partners = [dev(zhi=lax.rem(zh + i, 4), core=k) for i in (1, 3) for k in range(2)] + [dev(core=1 - c)]
    partners += [dev(dx=1), dev(dx=-1), dev(dx=2), dev(dy=1), dev(dy=-1)]
    partners += [dev(zlo=1 - zl, core=0), dev(zlo=1 - zl, core=1)]
    for partner in partners:
        pl.semaphore_signal(barrier, inc=1, device_id=partner, device_id_type=MESH)

    load_q.wait()
    load_p.wait()
    pre[...] = jnp.dot(qry[...], prec[...], preferred_element_type=jnp.float32).astype(jnp.bfloat16)
    pl.semaphore_wait(barrier, len(partners))

    mine = b.at[yi(0), rows(), half]

    def init(to, slot):
        return pltpu.make_async_remote_copy(
            src_ref=pre, dst_ref=mine, send_sem=init_s.at[slot], recv_sem=init_r.at[c],
            device_id=to, device_id_type=MESH)

    def init_got(h):
        dst = b.at[yi(0), rows(), pl.ds(pl.multiple_of(h * W, W), W)]
        pltpu.make_async_remote_copy(
            src_ref=pre, dst_ref=dst, send_sem=init_s.at[0], recv_sem=init_r.at[h],
            device_id=dev(), device_id_type=MESH).wait_recv()

    init_far = init(dev(zlo=1 - zl, core=1), 0)
    init_near = init(dev(core=1 - c), 1)
    init_own = pltpu.make_async_copy(pre, mine, load.at[3])
    init_far.start()

    @pl.when(c == 0)
    def _():
        init_own.start()

    @pl.when(c != 0)
    def _():
        init_near.start()

    load_a.wait()
    a_copy = pltpu.make_async_remote_copy(
        src_ref=a.at[c], dst_ref=a.at[c], send_sem=a_s, recv_sem=a_r,
        device_id=dev(core=1 - c), device_id_type=MESH)

    @pl.when(c == 0)
    def _():
        init_got(1)
        init_own.wait()

    @pl.when(c != 0)
    def _():
        init_got(0)
        init_got(1)

    def place(dy):
        ys = yi(dy)
        owner = 2 * serves + ys // 4
        return owner, lax.rem(ys // 2, 2), lax.rem(ys, 2), lax.rem(zh - owner + 4, 4)

    def height(unit):
        return ROWS if unit[1] is None else ROWS // 2

    def landing(unit, slot, j, part, kind):
        if unit[1] is None:
            return parts.at[slot, j, part], rs_r.at[kind, slot, j]
        return parts2.at[slot, unit[1], part], rs2_r.at[kind, slot, unit[1]]

    def part_of(unit, h):
        n = height(unit)
        return pl.ds(0, n) if h is None else pl.ds(pl.multiple_of(h * (n // 2), n // 2), n // 2)

    def owner_copy(unit, slot, h, kind):
        owner, core, j, _ = place(unit[0])
        i, part = UNITS.index(unit), part_of(unit, h)
        dst, sem = landing(unit, slot, j, part, kind)
        return pltpu.make_async_remote_copy(
            src_ref=stage.at[i, part], dst_ref=dst, send_sem=rs_s.at[kind, i], recv_sem=sem,
            device_id=dev(zhi=owner, core=core), device_id_type=MESH)

    def relay_copy(unit, h):
        i = UNITS.index(unit)
        return pltpu.make_async_remote_copy(
            src_ref=stage.at[i, part_of(unit, h)], dst_ref=relay.at[i, pl.ds(0, height(unit) // 2)],
            send_sem=mid_s.at[h, i], recv_sem=mid_r.at[i],
            device_id=dev(zhi=lax.rem(zh + (3, 1)[h], 4)), device_id_type=MESH)

    def local_copy(half, j):
        src, dst, k = (lstage.at[j], local.at[j], j) if half is None else (lstage2.at[half], local2.at[half], 2 + half)
        return pltpu.make_async_remote_copy(
            src_ref=src, dst_ref=dst, send_sem=l_s.at[k], recv_sem=l_r.at[k],
            device_id=dev(core=1 - c), device_id_type=MESH)

    def pair(half):
        low = x // 2 if half == 0 else 1 - x // 2
        return pl.ds(pl.multiple_of(low * CHUNK // 2, CHUNK // 2), CHUNK // 2)

    def chunk(unit):
        dy, half = unit
        i, n, ys = UNITS.index(unit), height(unit), yi(dy)
        these = slice(None) if half is None else pair(half)
        acc = lax.dot_general(a[0], b[ys, these, pl.ds(0, W)], NT, preferred_element_type=jnp.float32)
        acc += lax.dot_general(a[1], b[ys, these, pl.ds(W, W)], NT, preferred_element_type=jnp.float32)
        if half is not None:
            acc = jnp.concatenate([acc[:n], acc[n:]], axis=1)
        owner, core, j, away = place(dy)

        if unit in STRAIGHT:
            @pl.when(away != 0)
            def _():
                stage[i, :n] = acc.astype(jnp.bfloat16)
                owner_copy(unit, away - 1, None, 2).start()
        else:
            @pl.when(away == 2)
            def _():
                stage[i, :n] = acc.astype(jnp.bfloat16)
                relay_copy(unit, 0).start()
                relay_copy(unit, 1).start()

            for h, at in ((0, 1), (1, 3)):
                @pl.when(away == at)
                def _():
                    stage[i, part_of(unit, 1 - h)] = acc[(1 - h) * (n // 2):(2 - h) * (n // 2)].astype(jnp.bfloat16)
                    owner_copy(unit, 2 * h, 1 - h, 0).start()
                    hold[i, :n // 2] = acc[h * (n // 2):(h + 1) * (n // 2)]

        @pl.when(jnp.logical_and(away == 0, core == c))
        def _():
            if half is None:
                local[j] = acc
            else:
                local2[half] = acc

        @pl.when(jnp.logical_and(away == 0, core != c))
        def _():
            if half is None:
                lstage[j] = acc
            else:
                lstage2[half] = acc
            local_copy(half, j).start()

    def relayed(unit):
        i, n = UNITS.index(unit), height(unit)
        _, _, _, away = place(unit[0])

        @pl.when(lax.rem(away, 2) == 1)
        def _():
            h = away // 2
            relay_copy(unit, 0).wait_recv()
            stage[i, part_of(unit, h)] = (hold[i, :n // 2] + relay[i, :n // 2].astype(jnp.float32)).astype(jnp.bfloat16)
            owner_copy(unit, 2 * h, h, 1).start()

    names = list(messages())
    per_way = [name for name in names if name[0] in ("yy", "xy") and name[1] > 0]
    rest = [name for name in names if name[0] not in ("yy", "xy")]

    def tag(name):
        if name[0] in ("yy", "xy"):
            return per_way.index((name[0], 1, *name[2:])) + len(per_way) * minus(name[1])
        return 2 * len(per_way) + rest.index(name)

    def message(name):
        kind = name[0]
        if kind == "x1":
            p = PIECES[name[1]]
            return (0, 0, XCOLS), (0, p, XCOLS), dev(dx=-p)
        if kind == "xy":
            _, d, k, p = name
            place_x = PIECES[p] if k < 3 else (1 - minus(d)) * 2 * p + minus(d) * (1 - 2 * p) * (1 - 2 * lax.rem(x, 2))
            return (-d * k, place_x, XCOLS), (-d * (k + 1), place_x, XCOLS), dev(dy=mirror * d)
        if kind == "yy":
            _, d, k = name
            part = (0, QROWS) if k < 3 else (16 * minus(d), 16)
            return (-d * k, 0, YCOLS, *part), (-d * (k + 1), 0, YCOLS, *part), dev(dy=mirror * d)
        _, dy, d = name
        part = (0, QROWS) if kind == "yx" else (0, 16) if d > 0 else (16, 16)
        hops = 0 if kind == "yx" else 1
        return (dy, -d * hops, YCOLS, *part), (dy, -d * (hops + 1), YCOLS, *part), dev(dx=d)

    def sent():
        for cp in started:
            cp.wait_send()
        a_copy.wait_send()
        init_far.wait_send()

        @pl.when(c != 0)
        def _():
            init_near.wait_send()

    seen = set()
    for step, (kind, what, needs) in enumerate(plan()):
        if step == 20:
            a_copy.start()
        for name in needs:
            if name not in seen:
                seen.add(name)
                got(panel(*message(name)[1]), tag(name))
        if kind == "go":
            block, _, to = message(what)
            go(panel(*block), tag(what), to)
        elif kind == "chunk":
            if what == UNITS[0]:
                a_copy.wait_recv()
            chunk(what)
        elif kind == "relay":
            relayed(what)
        else:
            sent()

    for unit in UNITS:
        _, _, j, away = place(unit[0])
        if unit in STRAIGHT:
            @pl.when(away != 0)
            def _():
                owner_copy(unit, 0, None, 2).wait_send()
        else:
            @pl.when(away == 2)
            def _():
                relay_copy(unit, 0).wait_send()
                relay_copy(unit, 1).wait_send()

            @pl.when(lax.rem(away, 2) == 1)
            def _():
                owner_copy(unit, 0, 0, 0).wait_send()
                owner_copy(unit, 0, 0, 1).wait_send()

        _, core, j, _ = place(unit[0])

        @pl.when(jnp.logical_and(away == 0, core != c))
        def _():
            local_copy(unit[1], j).wait_send()

    def part_got(unit, slot, j, h, kind):
        part = part_of(unit, h)
        dst, sem = landing(unit, slot, j, part, kind)
        pltpu.make_async_remote_copy(
            src_ref=stage.at[0, part], dst_ref=dst, send_sem=rs_s.at[0, 0], recv_sem=sem,
            device_id=dev(), device_id_type=MESH).wait_recv()

    def collect(unit, j):
        @pl.when(zh // 2 != serves)
        def _():
            local_copy(unit[1], j).wait_recv()

        if unit in STRAIGHT:
            for slot in range(3):
                part_got(unit, slot, j, None, 2)
        else:
            for h in range(2):
                part_got(unit, 2 * h, j, 1 - h, 0)
                part_got(unit, 2 * h, j, h, 1)
        own, come = (local[j], parts.at[:, j]) if unit[1] is None else (local2[unit[1]], parts2.at[:, unit[1]])
        return own + sum(come[slot].astype(jnp.float32) for slot in ((0, 1, 2) if unit in STRAIGHT else (0, 2)))

    for j in range(2):
        far = lax.rem(4 * lax.rem(zh, 2) + 2 * c + j - y + 8, 8) == 4
        cols = slice(j * CHUNK, (j + 1) * CHUNK)

        @pl.when(jnp.logical_not(far))
        def _():
            o_ref[:, cols] = collect(UNITS[0], j)

        @pl.when(far)
        def _():
            mine, other = collect((4, 0), j), collect((4, 1), j)
            first = x // 2 == 0
            left, right = jnp.where(first, mine, other), jnp.where(first, other, mine)
            half = CHUNK // 2
            o_ref[:ROWS // 2, cols] = jnp.concatenate([left[:, :half], right[:, :half]], axis=1)
            o_ref[ROWS // 2:, cols] = jnp.concatenate([left[:, half:], right[:, half:]], axis=1)


def body(train_grads, query_grads, precond):
    bf16, f32 = jnp.bfloat16, jnp.float32
    dma = pltpu.SemaphoreType.DMA
    n_tags = len(messages())
    return pl.pallas_call(
        kernel,
        out_shape=pltpu.VMEM((ROWS, 2 * CHUNK), f32),
        in_specs=[pl.BlockSpec(memory_space=pltpu.HBM)] * 3,
        out_specs=pl.BlockSpec(memory_space=pltpu.VMEM),
        scratch_shapes=[
            pltpu.VMEM((W, W), bf16),
            pltpu.VMEM((QROWS, W), bf16),
            pltpu.VMEM((QROWS, W), bf16),
            pltpu.VMEM((2, ROWS, W), bf16),
            pltpu.VMEM((YS, CHUNK, 2 * W), bf16),
            pltpu.VMEM((len(UNITS), ROWS, CHUNK), bf16),
            pltpu.VMEM((len(UNITS), ROWS // 2, CHUNK), f32),
            pltpu.VMEM((len(UNITS), ROWS // 2, CHUNK), bf16),
            pltpu.VMEM((2, ROWS, CHUNK), f32),
            pltpu.VMEM((2, ROWS, CHUNK), f32),
            pltpu.VMEM((3, 2, ROWS, CHUNK), bf16),
            pltpu.VMEM((2, ROWS // 2, CHUNK), f32),
            pltpu.VMEM((2, ROWS // 2, CHUNK), f32),
            pltpu.VMEM((3, 2, ROWS // 2, CHUNK), bf16),
            dma((n_tags,)), dma((n_tags,)), dma((4,)), dma((2,)), dma((2,)), dma, dma,
            dma((3, len(UNITS))), dma((2, 3, 2)), dma((3, 3, 2)), dma((2, len(UNITS))), dma((len(UNITS),)), dma((4,)), dma((4,)),
        ],
        compiler_params=pltpu.CompilerParams(
            collective_id=0, has_side_effects=True, vmem_limit_bytes=60 * 1024 * 1024),
        cost_estimate=pl.CostEstimate(flops=2 * 2 * W * W * ROWS, bytes_accessed=4 << 20, transcendentals=0),
    )(train_grads, query_grads, precond)


def solution(mesh):
    placed = (P("train", "feat"), P("train", "feat"), P("feat", None))
    return jax.shard_map(
        body, mesh=mesh, in_specs=placed, out_specs=P("train", "feat"), check_vma=False
    )
```
